32 devices in a mesh: exp: 16 (over z, x, core), ten: 2 (over y).
Axes of the slice: x: 2, y: 2, z: 4, core: 2. Of those that a mesh axis runs over, the one named last changes fastest.
Arguments:
- tokens: bfloat16 [768, 4096], P('exp', 'ten'), may hold values from -6 to 6
- expert_ids: int32 [768, 8], P('exp'), may hold values from 0 to 15, all different within a row; in each aligned block of 48 rows (0 to 47, 48 to 95, ...) at most 30 rows name the same one
- combine_weights: float32 [768, 8], P('exp'), may hold values from 0.05 to 1
- gate_proj: bfloat16 [16, 1536, 4096], P('exp', 'ten'), may hold values from -0.09375 to 0.09375
- up_proj: bfloat16 [16, 1536, 4096], P('exp', 'ten'), may hold values from -0.09375 to 0.09375
- down_proj: bfloat16 [16, 1536, 4096], P('exp', 'ten'), may hold values from -0.15625 to 0.15625
Outputs:
- moe_out: bfloat16 [768, 4096], P('exp', 'ten')
The draws below stay inside these ranges and needn't reach their ends.
Inputs may be any that keep to these rules, and one draw needn't show every extreme that they name: `expert_ids`: each row names 8 different experts. Within each aligned block of 48 rows (the rows of one index of exp) no expert is named by more than 30 rows.
All inputs are finite; a program needn't handle non-finite values.
Results may differ from the reference program's by a relative error of at most 0.01.
Values may be sent and summed in bfloat16 or wider, within the bound.
No kernel may reach another device: no remote copies, remote signals or barrier semaphores. Data moves between devices by JAX's collectives and lax.ppermute only.
A program may use at most 128 MiB of HBM per device.

```python
import math
import jax
import jax.numpy as jnp
import numpy as np
from jax import lax

D = 4096
FF = 1536
TOP = 8
TOK_DEV = 48
EXPERTS = 16
CAP = 30
TOKENS = 768
N_TEN = 2


def levels(stream_key, extent, shards, least, high):
    gain = 1.0
    for dim, parts in shards:
        steps = jax.random.uniform(jax.random.fold_in(jax.random.fold_in(stream_key, 6), dim), (parts,), jnp.float32, least / len(shards), high / len(shards))
        gain = gain * jnp.repeat(jnp.exp(steps), extent[dim] // parts).reshape((-1,) + (1,) * (len(extent) - 1 - dim))
    return gain


def assign_block(stream_key, own, number, rows, number_of, top, limit, skew):
    order = jax.random.permutation(stream_key, number_of)
    crowded, ordinary = shares(number_of, rows * top, limit, skew, True), shares(number_of, rows * top, limit, skew, False)
    places = jnp.arange(number_of)

    def named(tallies, rotation):
        used = int((tallies > 0).sum())
        fixed = max(1, used // 4)
        moved = fixed + (places - fixed + rotation * (used - fixed)) % max(1, number_of - fixed)
        return jnp.zeros((number_of,), jnp.int32).at[order[jnp.where(places < fixed, places, moved)]].set(jnp.asarray(tallies, jnp.int32))

    tallies = jnp.where(number % 4 == 0, named(crowded, number // 4), named(ordinary, number - number // 4 - 1))
    mixed = jax.random.permutation(jax.random.fold_in(own, 3), number_of)
    donor, sink = mixed[0:number_of // 2 * 2:2], mixed[1:number_of // 2 * 2:2]
    slack = jnp.minimum(tallies[donor] - 1, limit - tallies[sink]) // 2
    slack = jnp.where((donor == order[0]) | (sink == order[0]) | (tallies[sink] == 0), 0, jnp.maximum(slack, 0))
    moved = jax.random.randint(jax.random.fold_in(own, 4), (number_of // 2,), 0, 1 << 20) % (slack + 1)
    tallies = tallies.at[donor].add(-moved).at[sink].add(moved)
    labels = jnp.searchsorted(jnp.cumsum(tallies), jnp.arange(rows * top), side="right").astype(jnp.int32)
    grid = labels.reshape(top, rows).T
    grid = grid[jax.random.permutation(jax.random.fold_in(own, 1), rows)]
    rotation = jax.random.randint(jax.random.fold_in(own, 2), (rows, 1), 0, top)
    return jnp.take_along_axis(grid, (jnp.arange(top)[None, :] + rotation) % top, axis=1)


def shares(amount, total, limit, skew, full):
    portions = [(1 << 20) // math.isqrt(grade ** skew) + 1 for grade in range(1, amount + 1)]
    largest = limit if full else min(limit, max(-(-total // amount), total * portions[0] // sum(portions)))
    least = 1 if total - largest >= amount - 1 else 0
    counts, rest = [largest] + [least] * (amount - 1), total - largest - least * (amount - 1)
    while rest > 0:
        movable = [i for i in range(1, amount) if counts[i] < largest] or [i for i in range(1, amount) if counts[i] < limit]
        whole, left = sum([portions[i] for i in movable]), rest
        for i in movable:
            extra = min(limit - counts[i], max(1, left * portions[i] // whole), rest)
            counts[i] = counts[i] + extra
            rest = rest - extra
    return np.array(counts)


def scatter_about(rng, dims, scale, limit, cuts=(), kind=jnp.bfloat16):
    gain = levels(rng, dims, cuts, -0.22, 0.18) if cuts else 1.0
    values = jax.random.normal(rng, dims, jnp.float32) * scale * gain
    return jnp.minimum(jnp.maximum(values, -limit), limit).astype(kind)


def setup_inputs(seed: int = 0) -> dict:
    seeds = jax.random.split(jax.random.key(seed), 7)
    tokens = scatter_about(seeds[0], (TOKENS, D), 1.0, 6.0, ((0, 16), (1, 2)))
    expert_ids_keys = jax.random.split(jax.random.fold_in(seeds[1], 1), TOKENS // TOK_DEV)
    expert_ids_turns = jax.random.permutation(jax.random.fold_in(seeds[1], 3), TOKENS // TOK_DEV)
    expert_ids = jax.vmap(lambda own, number: assign_block(jax.random.fold_in(seeds[1], 2), own, number, TOK_DEV, EXPERTS, TOP, CAP, 1))(expert_ids_keys, expert_ids_turns).reshape((TOKENS, TOP))
    combine_weights = jnp.clip(jnp.exp(math.log(1.0) - 2.9957323 * jax.random.uniform(seeds[2], (TOKENS, TOP), jnp.float32) ** levels(seeds[2], (TOKENS, TOP), ((0, 16),), -0.2, 0.2)), 0.05, 1.0)
    gate_proj = scatter_about(seeds[3], (EXPERTS, FF, D), D ** -0.5, 0.09375, ((0, 16), (1, 2)))
    up_proj = scatter_about(seeds[4], (EXPERTS, FF, D), D ** -0.5, 0.09375, ((0, 16), (1, 2)))
    down_proj = scatter_about(seeds[5], (EXPERTS, FF, D), FF ** -0.5, 0.15625, ((0, 16), (1, 2)))
    return {"tokens": tokens, "expert_ids": expert_ids, "combine_weights": combine_weights, "gate_proj": gate_proj, "up_proj": up_proj, "down_proj": down_proj}


def reference(tokens, expert_ids, combine_weights, gate_proj, up_proj, down_proj):
    blocks = TOKENS // TOK_DEV
    slot_rows = blocks * CAP
    slice_width = FF // N_TEN
    grouped = expert_ids.reshape(blocks, TOK_DEV * TOP)
    matches = (grouped[:, :, None] == jnp.arange(EXPERTS, dtype=jnp.int32)[None, None, :]).astype(jnp.int32)
    earlier = jnp.cumsum(matches, axis=1) - matches
    slots = jnp.sum(earlier * matches, axis=2).astype(jnp.int32)
    positions = (jnp.arange(blocks, dtype=jnp.int32)[:, None] * CAP + slots).reshape(-1).astype(jnp.int32)
    flattened = expert_ids.reshape(-1)
    weights_flat = combine_weights.reshape(-1)
    owners = (jnp.arange(TOKENS * TOP, dtype=jnp.int32) // TOP).astype(jnp.int32)

    def one_expert(running, expert):
        chosen = flattened == expert
        targets = jnp.where(chosen, positions, slot_rows).astype(jnp.int32)
        sources = jnp.zeros((slot_rows,), jnp.int32).at[targets].set(owners, mode="drop")
        filled = jnp.zeros((slot_rows,), jnp.float32).at[targets].set(1.0, mode="drop")
        weight_slot = jnp.zeros((slot_rows,), jnp.float32).at[targets].set(weights_flat, mode="drop")
        gathered = jnp.where(filled[:, None] > 0.5, tokens[sources], jnp.zeros((), jnp.bfloat16))
        gate_sum = jnp.dot(gathered, gate_proj[expert].T, preferred_element_type=jnp.float32)
        up_sum = jnp.dot(gathered, up_proj[expert].T, preferred_element_type=jnp.float32)
        hidden = (jax.nn.silu(gate_sum) * up_sum).astype(jnp.bfloat16)
        pieces = jnp.einsum("rjf,jfd->jrd", hidden.reshape(slot_rows, N_TEN, slice_width).astype(jnp.float32),
                            down_proj[expert].reshape(N_TEN, slice_width, D).astype(jnp.float32))
        expert_out = jnp.sum(pieces.astype(jnp.bfloat16).astype(jnp.float32), axis=0)
        running = running.at[sources].add(weight_slot[:, None] * expert_out)
        return running, None

    running, unused = lax.scan(one_expert, jnp.zeros((TOKENS, D), jnp.float32), jnp.arange(EXPERTS, dtype=jnp.int32))
    return running.astype(jnp.bfloat16)
```

```python
import functools

import jax
import jax.numpy as jnp
from jax import lax
from jax.experimental import pallas as pl
from jax.experimental.pallas import tpu as pltpu
from jax.sharding import Mesh, PartitionSpec as P

BF = jnp.bfloat16
F32 = jnp.float32
NT = (((1,), (1,)), ((), ()))


def block_of(extent, want):
    size = min(extent, want)
    while extent % size:
        size //= 2
    return size


def ffn_kernel(steps, halves, pieces, own_cols, sc, *refs):
    n = pieces
    own, oth = refs[:n], refs[n : 2 * n]
    wg, wu, wd = refs[2 * n : 2 * n + 3]
    outs = refs[2 * n + 3 : -3]
    x_s, h_s, w_s = refs[-3:]
    i = pl.program_id(0)
    rows = own[0].shape[0]
    n_hidden, n_down = steps

    @pl.when(i == 0)
    def _():
        mine = pl.multiple_of(sc[0] * own_cols, 128)
        other = pl.multiple_of((1 - sc[0]) * own_cols, 128)
        lane = lax.broadcasted_iota(jnp.int32, (rows, 128), 1)
        chosen = (lane == sc[1]) | (lane == sc[1] + 64)
        for j in range(n):
            r = pl.ds(j * rows, rows)
            x_s[r, pl.ds(mine, own_cols)] = own[j][:, :own_cols]
            x_s[r, pl.ds(other, own_cols)] = oth[j][:, :own_cols]
            tail = own[j][:, own_cols:].astype(F32)
            w_s[r, :] = jnp.broadcast_to(
                jnp.sum(jnp.where(chosen, tail, 0.0), axis=1, keepdims=True), (rows, 128)
            )

    @pl.when(i < n_hidden)
    def _():
        x = x_s[...]
        g = lax.dot_general(x, wg[...], NT, preferred_element_type=F32)
        u = lax.dot_general(x, wu[...], NT, preferred_element_type=F32)
        h_s[i] = (g / (1.0 + jnp.exp(-g)) * u * w_s[:, :1]).astype(BF)

    def down(group):
        h = jnp.concatenate([h_s[k] for k in range(n_hidden)], axis=1)
        o = jnp.dot(h, wd[...], preferred_element_type=F32).astype(BF)
        per = n // len(group) * rows
        for k, ref in enumerate(group):
            ref[...] = o[k * per : (k + 1) * per]

    half = len(outs) // 2

    @pl.when((i >= n_hidden) & (i < n_hidden + n_down // 2))
    def _():
        down(outs[:half])

    @pl.when(i >= n_hidden + n_down // 2)
    def _():
        down(outs[half:])


def ffn(own, oth, sc, wg, wu, wd):
    n = len(own)
    rows, wide = own[0].shape
    cols = wide - 128
    ff, d = wg.shape
    fb, nb = block_of(ff, 256), block_of(cols, 1024)
    nh, nd = ff // fb, d // nb
    hd = nd // 2
    total = n * rows
    piece = pl.BlockSpec((rows, wide), lambda i, s: (0, 0))
    up = pl.BlockSpec((fb, d), lambda i, s: (jnp.minimum(i, nh - 1), 0))

    def down_col(i, s):
        return (0, (s[0] * hd + jnp.maximum(i - nh, 0)) % nd)

    out_own = pl.BlockSpec((total // 2, nb), lambda i, s: (0, jnp.clip(i - nh, 0, hd - 1)))
    out_oth = pl.BlockSpec((total // 2, nb), lambda i, s: (0, jnp.clip(i - nh - hd, 0, hd - 1)))
    shape = jax.ShapeDtypeStruct((total // 2, cols), BF)
    return pl.pallas_call(
        functools.partial(ffn_kernel_entry, (nh, nd), n, cols),
        grid_spec=pltpu.PrefetchScalarGridSpec(
            num_scalar_prefetch=1,
            grid=(nh + nd,),
            in_specs=[piece] * (2 * n) + [up, up, pl.BlockSpec((ff, nb), down_col)],
            out_specs=[out_own, out_own, out_oth, out_oth],
            scratch_shapes=[
                pltpu.VMEM((total, d), BF),
                pltpu.VMEM((nh, total, fb), BF),
                pltpu.VMEM((total, 128), F32),
            ],
        ),
        out_shape=[shape] * 4,
        compiler_params=pltpu.CompilerParams(vmem_limit_bytes=48 << 20),
        cost_estimate=pl.CostEstimate(
            flops=6 * total * ff * d, bytes_accessed=6 * ff * d + 4 * total * d, transcendentals=total * ff
        ),
        name="ffn",
    )(sc, *own, *oth, wg, wu, wd)


def ffn_kernel_entry(steps, pieces, cols, sc, *refs):
    ffn_kernel(steps, 4, pieces, cols, sc, *refs)


def dense_weights(expert_ids, combine_weights, experts):
    hits = expert_ids[:, :, None] == jnp.arange(experts, dtype=jnp.int32)
    return jnp.sum(jnp.where(hits, combine_weights[:, :, None], 0.0), axis=1)


def on_device(tokens, expert_ids, combine_weights, gate_proj, up_proj, down_proj):
    held, cols = tokens.shape
    nz, nx = lax.axis_size("z"), lax.axis_size("x")
    experts = nz * nx * 2
    wg, wu, wd = gate_proj[0], up_proj[0], down_proj[0]
    z, x, c, y = (lax.axis_index(a) for a in ("z", "x", "c", "y"))
    sc = jnp.stack([y, (z * nx + x) * 2 + c]).astype(jnp.int32)

    swap = [(0, 1), (1, 0)]
    px = lambda a: lax.ppermute(a, "x", swap)
    py = lambda a: lax.ppermute(a, "y", swap)
    pc = lambda a: lax.ppermute(a, "c", swap)
    ahead = lambda a, k: lax.ppermute(a, "z", [(i, (i + k) % nz) for i in range(nz)])

    w = dense_weights(expert_ids, combine_weights, experts)
    hi = w.astype(BF)
    lo = (w - hi.astype(F32)).astype(BF)
    pad = jnp.zeros((held, 64 - experts), BF)
    t = [jnp.concatenate([tokens, hi, pad, lo, pad], axis=1)]

    for k in range(1, nz):
        t.append(ahead(t[-1], 1))
    xs = [px(a) for a in t]
    ys = [py(a) for a in t]
    early, late = list(range(nz // 2)), list(range(nz // 2, nz))
    ds = [py(xs[k]) for k in early] + [px(ys[k]) for k in late]

    first = ffn(t + [pc(a) for a in t], ys + [pc(a) for a in ys], sc, wg, wu, wd)
    last = ffn(xs + [pc(a) for a in xs], ds + [pc(a) for a in ds], sc, wg, wu, wd)

    def plane_sum(own_c, oth_c):
        s = own_c.astype(F32) + pc(oth_c).astype(F32)
        return s.reshape(nz, held, cols)

    s1_own, s1_oth = plane_sum(first[0], first[1]), plane_sum(first[2], first[3])
    s2_own, s2_oth = plane_sum(last[0], last[1]), plane_sum(last[2], last[3])

    ga, gb = [1, 3], [2, 0]
    done = {}
    ry1 = {k: py(s1_oth[k].astype(BF)) for k in gb}
    ry2 = {k: py(s2_oth[k].astype(BF)) for k in gb}
    for k in ga:
        r = px(jnp.stack([s2_own[k], s2_oth[k]]).astype(BF)).astype(F32)
        back = py((s1_oth[k] + r[1]).astype(BF)).astype(F32)
        done[k] = s1_own[k] + r[0] + back
    for k in gb:
        v = px((s2_own[k] + ry2[k].astype(F32)).astype(BF)).astype(F32)
        done[k] = s1_own[k] + ry1[k].astype(F32) + v
    total = done[0]
    for k in range(1, nz):
        total = total + ahead(done[k].astype(BF), nz - k).astype(F32)
    return total.astype(BF)


def on_device_any(tokens, expert_ids, combine_weights, gate_proj, up_proj, down_proj):
    groups = lax.axis_size("exp")
    held, cols = tokens.shape
    local = gate_proj.shape[0]
    w = lax.all_gather(dense_weights(expert_ids, combine_weights, groups * local), "exp", axis=0, tiled=True)
    rows = lax.all_gather(lax.all_gather(tokens, "ten", axis=1, tiled=True), "exp", axis=0, tiled=True)
    total = jnp.zeros((rows.shape[0], rows.shape[1]), F32)
    for j in range(local):
        g = lax.dot_general(rows, gate_proj[j], NT, preferred_element_type=F32)
        u = lax.dot_general(rows, up_proj[j], NT, preferred_element_type=F32)
        mine = jnp.take(w, lax.axis_index("exp") * local + j, axis=1)[:, None]
        h = (jax.nn.silu(g) * u * mine).astype(BF)
        total = total + jnp.dot(h, down_proj[j], preferred_element_type=F32)
    part = lax.psum_scatter(total.astype(BF), "exp", scatter_dimension=0, tiled=True)
    return lax.psum_scatter(part, "ten", scatter_dimension=1, tiled=True).astype(BF)


def solution(mesh):
    sizes = (mesh.shape["exp"], mesh.shape["ten"])
    if sizes == (16, 2):
        mesh = Mesh(mesh.devices.reshape(4, 2, 2, 2), ("z", "x", "c", "y"))
        exp, ten, body = ("z", "x", "c"), "y", on_device
    else:
        exp, ten, body = "exp", "ten", on_device_any
    return jax.shard_map(
        body,
        mesh=mesh,
        in_specs=(
            P(exp, ten),
            P(exp, None),
            P(exp, None),
            P(exp, ten, None),
            P(exp, ten, None),
            P(exp, ten, None),
        ),
        out_specs=P(exp, ten),
        check_vma=False,
    )
```

```python
import functools

import jax
import jax.numpy as jnp
from jax import lax
from jax.experimental import pallas as pl
from jax.experimental.pallas import tpu as pltpu
from jax.sharding import Mesh, PartitionSpec as P

BF = jnp.bfloat16
F32 = jnp.float32
NT = (((1,), (1,)), ((), ()))


UNITS = 8


def ffn_kernel(layout, cols, *refs):
    sc, refs = refs[0], refs[1:]
    pieces, (wg, wu, wd) = refs[:8], refs[8:11]
    outs, (x_s, h_s, w_s) = refs[11:15], refs[15:]
    rows = x_s.shape[0] // UNITS
    ff, d = wg.shape
    fb, nb = 256, 512
    mine = pl.multiple_of(sc[0] * cols, 128)
    other = pl.multiple_of((1 - sc[0]) * cols, 128)
    lane = lax.broadcasted_iota(jnp.int32, (rows, 128), 1)
    chosen = (lane == sc[1]) | (lane == sc[1] + 64)
    for b, (p, i, q, j) in enumerate(layout):
        r = pl.ds(b * rows, rows)
        x_s[r, pl.ds(mine, cols)] = pieces[p][i * rows : (i + 1) * rows, :cols]
        x_s[r, pl.ds(other, cols)] = pieces[q][j * rows : (j + 1) * rows, :cols]
        tail = pieces[p][i * rows : (i + 1) * rows, cols:].astype(F32)
        w_s[r, :] = jnp.broadcast_to(jnp.sum(jnp.where(chosen, tail, 0.0), axis=1, keepdims=True), (rows, 128))
    for f in range(0, ff, fb):
        x = x_s[...]
        g = lax.dot_general(x, wg[pl.ds(f, fb), :], NT, preferred_element_type=F32)
        u = lax.dot_general(x, wu[pl.ds(f, fb), :], NT, preferred_element_type=F32)
        h_s[:, pl.ds(f, fb)] = (g / (1.0 + jnp.exp(-g)) * u * w_s[:, :1]).astype(BF)
    for n in range(0, 2 * cols, nb):
        far = n >= cols
        off = n - cols if far else n
        at = pl.multiple_of((other if far else mine) + off, 128)
        o = jnp.dot(h_s[...], wd[:, pl.ds(at, nb)], preferred_element_type=F32).astype(BF)
        for b in range(UNITS):
            core, plane, side = b // 4, b // 2 % 2, b % 2
            sends, unit = (side, int(far)) if plane == 0 else (int(far), side)
            out = outs[(0 if sends else 2) + core]
            k = (plane * 2 + unit) * rows
            out[k : k + rows, off : off + nb] = o[b * rows : (b + 1) * rows]


def ffn(sc, pieces, layout, cols, wg, wu, wd):
    ff, d = wg.shape
    rows = pieces[0].shape[0] // 2
    total = UNITS * rows
    vmem = pl.BlockSpec(memory_space=pltpu.VMEM)
    return pl.pallas_call(
        functools.partial(ffn_kernel, layout, cols),
        in_specs=[pl.BlockSpec(memory_space=pltpu.SMEM)] + [vmem] * 11,
        out_specs=[vmem] * 4,
        out_shape=[pltpu.VMEM((4 * rows, cols), BF)] * 4,
        scratch_shapes=[
            pltpu.VMEM((total, d), BF),
            pltpu.VMEM((total, ff), BF),
            pltpu.VMEM((total, 128), F32),
        ],
        compiler_params=pltpu.CompilerParams(vmem_limit_bytes=16 << 20),
        cost_estimate=pl.CostEstimate(
            flops=6 * total * ff * d, bytes_accessed=4 * total * d, transcendentals=total * ff
        ),
        name="ffn",
    )(sc, *pieces, wg, wu, wd)


def dense_weights(expert_ids, combine_weights, experts):
    hits = expert_ids[:, :, None] == jnp.arange(experts, dtype=jnp.int32)
    return jnp.sum(jnp.where(hits, combine_weights[:, :, None], 0.0), axis=1)


def on_device(tokens, expert_ids, combine_weights, gate_proj, up_proj, down_proj):
    held, cols = tokens.shape
    nz, nx = lax.axis_size("z"), lax.axis_size("x")
    experts = nz * nx * 2
    z, x, c, y = (lax.axis_index(a) for a in ("z", "x", "c", "y"))
    sc = jnp.stack([y, (z * nx + x) * 2 + c]).astype(jnp.int32)
    weights = (gate_proj[0], up_proj[0], down_proj[0])

    swap = [(0, 1), (1, 0)]
    px = lambda a: lax.ppermute(a, "x", swap)
    py = lambda a: lax.ppermute(a, "y", swap)
    pc = lambda a: lax.ppermute(a, "c", swap)
    pz = lambda a, k: lax.ppermute(a, "z", [(i, i ^ k) for i in range(nz)])

    w = dense_weights(expert_ids, combine_weights, experts)
    hi = w.astype(BF)
    lo = (w - hi.astype(F32)).astype(BF)
    pad = jnp.zeros((held, 64 - experts), BF)
    t0 = jnp.concatenate([tokens, hi, pad, lo, pad], axis=1)

    t1, t3 = pz(t0, 1), pz(t0, 3)
    t2 = pz(t3, 1)

    def gather(a, b):
        ma, mb = jnp.concatenate([a, py(a)]), jnp.concatenate([b, px(b)])
        na, nb = px(ma), py(mb)
        return [ma, na, mb, nb, pc(ma), pc(na), pc(mb), pc(nb)]

    layout = []
    for core in (0, 4):
        layout += [(core, 0, core, 1), (core + 1, 0, core + 1, 1)]
        layout += [(core + 2, 0, core + 3, 0), (core + 2, 1, core + 3, 1)]

    def scatter(parts):
        send, send_c, keep, keep_c = parts
        s = (send.astype(F32) + pc(send_c).astype(F32)).astype(BF)
        k = (keep.astype(F32) + pc(keep_c).astype(F32)).reshape(4, held, cols)
        ra = px(s[: 2 * held]).astype(F32).reshape(2, held, cols)
        rb = py(s[2 * held :]).astype(F32).reshape(2, held, cols)
        back_a = py((k[1] + ra[1]).astype(BF)).astype(F32)
        back_b = px((k[3] + rb[1]).astype(BF)).astype(F32)
        return k[0] + ra[0] + back_a, k[2] + rb[0] + back_b

    first = ffn(sc, gather(t0, t1), layout, cols, *weights)
    last = ffn(sc, gather(t3, t2), layout, cols, *weights)
    u0, u1 = scatter(first)
    u3, u2 = scatter(last)
    total = u0 + pz(u1.astype(BF), 1).astype(F32)
    total = total + pz(u3.astype(BF), 3).astype(F32) + pz(u2.astype(BF), 2).astype(F32)
    return total.astype(BF)


def on_device_any(tokens, expert_ids, combine_weights, gate_proj, up_proj, down_proj):
    groups = lax.axis_size("exp")
    held, cols = tokens.shape
    local = gate_proj.shape[0]
    w = lax.all_gather(dense_weights(expert_ids, combine_weights, groups * local), "exp", axis=0, tiled=True)
    rows = lax.all_gather(lax.all_gather(tokens, "ten", axis=1, tiled=True), "exp", axis=0, tiled=True)
    total = jnp.zeros((rows.shape[0], rows.shape[1]), F32)
    for j in range(local):
        g = lax.dot_general(rows, gate_proj[j], NT, preferred_element_type=F32)
        u = lax.dot_general(rows, up_proj[j], NT, preferred_element_type=F32)
        mine = jnp.take(w, lax.axis_index("exp") * local + j, axis=1)[:, None]
        h = (jax.nn.silu(g) * u * mine).astype(BF)
        total = total + jnp.dot(h, down_proj[j], preferred_element_type=F32)
    part = lax.psum_scatter(total.astype(BF), "exp", scatter_dimension=0, tiled=True)
    return lax.psum_scatter(part, "ten", scatter_dimension=1, tiled=True).astype(BF)


def solution(mesh):
    sizes = (mesh.shape["exp"], mesh.shape["ten"])
    if sizes == (16, 2):
        mesh = Mesh(mesh.devices.reshape(4, 2, 2, 2), ("z", "x", "c", "y"))
        exp, ten, body = ("z", "x", "c"), "y", on_device
    else:
        exp, ten, body = "exp", "ten", on_device_any
    return jax.shard_map(
        body,
        mesh=mesh,
        in_specs=(
            P(exp, ten),
            P(exp, None),
            P(exp, None),
            P(exp, ten, None),
            P(exp, ten, None),
            P(exp, ten, None),
        ),
        out_specs=P(exp, ten),
        check_vma=False,
    )
```

```python
import functools

import jax
import jax.numpy as jnp
from jax import lax
from jax.experimental import pallas as pl
from jax.experimental.pallas import tpu as pltpu
from jax.sharding import Mesh, PartitionSpec as P

BF = jnp.bfloat16
F32 = jnp.float32
NT = (((1,), (1,)), ((), ()))


STEPS = 3
UNITS = 8


def ffn_kernel(layout, cols, fresh, waits, *refs):
    refs = refs[waits:]
    sc, refs = refs[0], refs[1:]
    pieces, given, outs, refs = refs[:8], refs[8:11], refs[11:15], refs[15:]
    held = given
    if fresh:
        held, refs = refs[:3], refs[3:]
    wg, wu, wd = held
    x_s, h_s, w_s = refs[:3]
    rows = x_s.shape[0] // UNITS
    ff, d = wg.shape
    fb, nb = ff // STEPS, 512

    def stream(k, step):
        part = pl.ds(step * fb, fb)
        return pltpu.make_async_copy(given[k].at[part], held[k].at[part], refs[3].at[k * STEPS + step])

    if fresh:
        for step in range(STEPS):
            stream(0, step).start()
            stream(1, step).start()
        for step in range(STEPS):
            stream(2, step).start()
    mine = pl.multiple_of(sc[0] * cols, 128)
    other = pl.multiple_of((1 - sc[0]) * cols, 128)
    lane = lax.broadcasted_iota(jnp.int32, (rows, 128), 1)
    chosen = (lane == sc[1]) | (lane == sc[1] + 64)
    for b, (p, i, q, j) in enumerate(layout):
        r = pl.ds(b * rows, rows)
        x_s[r, pl.ds(mine, cols)] = pieces[p][i * rows : (i + 1) * rows, :cols]
        x_s[r, pl.ds(other, cols)] = pieces[q][j * rows : (j + 1) * rows, :cols]
        tail = pieces[p][i * rows : (i + 1) * rows, cols:].astype(F32)
        w_s[r, :] = jnp.broadcast_to(jnp.sum(jnp.where(chosen, tail, 0.0), axis=1, keepdims=True), (rows, 128))
    for step in range(STEPS):
        f = step * fb
        if fresh:
            stream(0, step).wait()
            stream(1, step).wait()
        x = x_s[...]
        g = lax.dot_general(x, wg[pl.ds(f, fb), :], NT, preferred_element_type=F32)
        u = lax.dot_general(x, wu[pl.ds(f, fb), :], NT, preferred_element_type=F32)
        h_s[:, pl.ds(f, fb)] = (g / (1.0 + jnp.exp(-g)) * u * w_s[:, :1]).astype(BF)
    if fresh:
        for step in range(STEPS):
            stream(2, step).wait()
    for n in range(0, 2 * cols, nb):
        far = int(n >= cols)
        off = n - cols if far else n
        at = pl.multiple_of((other if far else mine) + off, 128)
        o = jnp.dot(h_s[...], wd[:, pl.ds(at, nb)], preferred_element_type=F32).astype(BF)
        for b in range(UNITS):
            core, plane, side = b // 4, b // 2 % 2, b % 2
            if side and far:
                group, unit = 0, plane
            elif side != far:
                group, unit = (0, 2 + plane) if side != plane else (2, plane)
            else:
                group, unit = 2, 2 + plane
            k = unit * rows
            outs[group + core][k : k + rows, off : off + nb] = o[b * rows : (b + 1) * rows]


def ffn(sc, pieces, layout, cols, weights, fresh, first_of_all):
    ff, d = weights[0].shape
    total = len(layout) * pieces[1].shape[0]
    vmem = pl.BlockSpec(memory_space=pltpu.VMEM)
    out = [pltpu.VMEM((total // 2, cols), BF)] * 4
    scratch = [pltpu.VMEM((total, d), BF), pltpu.VMEM((total, ff), BF), pltpu.VMEM((total, 128), F32)]
    if fresh:
        out += [pltpu.VMEM(a.shape, BF) for a in weights]
        scratch.append(pltpu.SemaphoreType.DMA((3 * STEPS,)))
    return pl.pallas_call(
        functools.partial(ffn_kernel, layout, cols, fresh, len(first_of_all)),
        in_specs=[pl.BlockSpec(memory_space=pl.ANY)] * len(first_of_all)
        + [pl.BlockSpec(memory_space=pltpu.SMEM)]
        + [vmem] * 8
        + [pl.BlockSpec(memory_space=pltpu.HBM) if fresh else vmem] * 3,
        out_specs=[vmem] * len(out),
        out_shape=out,
        scratch_shapes=scratch,
        compiler_params=pltpu.CompilerParams(vmem_limit_bytes=(36 if fresh else 8) << 20),
        cost_estimate=pl.CostEstimate(
            flops=6 * total * ff * d, bytes_accessed=6 * ff * d + 4 * total * d, transcendentals=total * ff
        ),
        name="ffn",
    )(*first_of_all, sc, *pieces, *weights)


def dense_weights(expert_ids, combine_weights, experts):
    hits = expert_ids[:, :, None] == jnp.arange(experts, dtype=jnp.int32)
    return jnp.sum(jnp.where(hits, combine_weights[:, :, None], 0.0), axis=1)


def on_device(tokens, expert_ids, combine_weights, gate_proj, up_proj, down_proj):
    held, cols = tokens.shape
    nz, nx = lax.axis_size("z"), lax.axis_size("x")
    experts = nz * nx * 2
    z, x, c, y = (lax.axis_index(a) for a in ("z", "x", "c", "y"))
    sc = jnp.stack([y, (z * nx + x) * 2 + c]).astype(jnp.int32)
    weights = (gate_proj[0], up_proj[0], down_proj[0])

    swap = [(0, 1), (1, 0)]
    px = lambda a: lax.ppermute(a, "x", swap)
    py = lambda a: lax.ppermute(a, "y", swap)
    pc = lambda a: lax.ppermute(a, "c", swap)
    pz = lambda a, k: lax.ppermute(a, "z", [(i, i ^ k) for i in range(nz)])

    w = dense_weights(expert_ids, combine_weights, experts)
    hi = w.astype(BF)
    lo = (w - hi.astype(F32)).astype(BF)
    pad = jnp.zeros((held, 64 - experts), BF)
    t0 = jnp.concatenate([tokens, hi, pad, lo, pad], axis=1)

    t1, t3 = pz(t0, 1), pz(t0, 3)
    t2 = pz(t3, 1)

    def gather(a, b):
        xa, yb, ya, xb = px(a), py(b), py(a), px(b)
        da, db = py(xa), px(yb)
        return [jnp.concatenate([a, xa, ya]), da, jnp.concatenate([b, xb, yb]), db]

    layout = []
    for core in (0, 4):
        for plane in (core, core + 2):
            layout += [(plane, 0, plane, 2), (plane, 1, plane + 1, 0)]

    def core_sum(parts):
        send, send_c, keep, keep_c = parts
        s = (send.astype(F32) + pc(send_c).astype(F32)).astype(BF).reshape(4, held, cols)
        k = (keep.astype(F32) + pc(keep_c).astype(F32)).reshape(4, held, cols)
        return s, k

    def scatter(s, k):
        ra, rb, qa, qb = px(s[0]), py(s[1]), px(s[2]), py(s[3])
        back_a = py((k[0] + ra.astype(F32)).astype(BF)).astype(F32)
        back_b = px((k[1] + rb.astype(F32)).astype(BF)).astype(F32)
        return k[2] + qa.astype(F32) + back_a, k[3] + qb.astype(F32) + back_b

    near, far = gather(t0, t1), gather(t3, t2)
    near_c = [pc(a) for a in near]
    far_c = [pc(a) for a in far]
    *first, wg, wu, wd = ffn(sc, far + far_c, layout, cols, weights, True, near_c)
    s, k = core_sum(first)
    last = ffn(sc, near + near_c, layout, cols, (wg, wu, wd), False, [s])
    u3, u2 = scatter(s, k)
    u0, u1 = scatter(*core_sum(last))
    total = u0 + pz(u3.astype(BF), 3).astype(F32) + pz(u2.astype(BF), 2).astype(F32)
    total = total + pz(u1.astype(BF), 1).astype(F32)
    return total.astype(BF)


def on_device_any(tokens, expert_ids, combine_weights, gate_proj, up_proj, down_proj):
    groups = lax.axis_size("exp")
    held, cols = tokens.shape
    local = gate_proj.shape[0]
    w = lax.all_gather(dense_weights(expert_ids, combine_weights, groups * local), "exp", axis=0, tiled=True)
    rows = lax.all_gather(lax.all_gather(tokens, "ten", axis=1, tiled=True), "exp", axis=0, tiled=True)
    total = jnp.zeros((rows.shape[0], rows.shape[1]), F32)
    for j in range(local):
        g = lax.dot_general(rows, gate_proj[j], NT, preferred_element_type=F32)
        u = lax.dot_general(rows, up_proj[j], NT, preferred_element_type=F32)
        mine = jnp.take(w, lax.axis_index("exp") * local + j, axis=1)[:, None]
        h = (jax.nn.silu(g) * u * mine).astype(BF)
        total = total + jnp.dot(h, down_proj[j], preferred_element_type=F32)
    part = lax.psum_scatter(total.astype(BF), "exp", scatter_dimension=0, tiled=True)
    return lax.psum_scatter(part, "ten", scatter_dimension=1, tiled=True).astype(BF)


def solution(mesh):
    sizes = (mesh.shape["exp"], mesh.shape["ten"])
    if sizes == (16, 2):
        mesh = Mesh(mesh.devices.reshape(4, 2, 2, 2), ("z", "x", "c", "y"))
        exp, ten, body = ("z", "x", "c"), "y", on_device
    else:
        exp, ten, body = "exp", "ten", on_device_any
    return jax.shard_map(
        body,
        mesh=mesh,
        in_specs=(
            P(exp, ten),
            P(exp, None),
            P(exp, None),
            P(exp, ten, None),
            P(exp, ten, None),
            P(exp, ten, None),
        ),
        out_specs=P(exp, ten),
        check_vma=False,
    )
```

```python
import functools

import jax
import jax.numpy as jnp
from jax import lax
from jax.experimental import pallas as pl
from jax.experimental.pallas import tpu as pltpu
from jax.sharding import Mesh, PartitionSpec as P

BF = jnp.bfloat16
F32 = jnp.float32
NT = (((1,), (1,)), ((), ()))


STEPS = 3
BLOCKS = 4
UNITS = 8


def ffn_kernel(layout, cols, fresh, waits, count, *refs):
    refs = refs[waits:]
    sc, refs = refs[0], refs[1:]
    pieces, given, outs, refs = refs[:count], refs[count : count + 3], refs[count + 3 : count + 7], refs[count + 7 :]
    held = given
    if fresh:
        held, refs = refs[:3], refs[3:]
    wg, wu, wd = held
    x_s, h_s, w_s = refs[:3]
    rows = x_s.shape[0] // UNITS
    ff, d = wg.shape
    fb, nb = ff // STEPS, 512

    def stream(k, step):
        part = pl.ds(step * fb, fb)
        return pltpu.make_async_copy(given[k].at[part], held[k].at[part], refs[3].at[k * STEPS + step])

    if fresh:
        for step in range(STEPS):
            stream(0, step).start()
            stream(1, step).start()
        for step in range(STEPS):
            stream(2, step).start()
    mine = pl.multiple_of(sc[0] * cols, 128)
    other = pl.multiple_of((1 - sc[0]) * cols, 128)
    lane = lax.broadcasted_iota(jnp.int32, (rows, 128), 1)
    chosen = (lane == sc[1]) | (lane == sc[1] + 64)
    for b, (p, i, q, j) in enumerate(layout):
        r = pl.ds(b * rows, rows)
        x_s[r, pl.ds(mine, cols)] = pieces[p][i * rows : (i + 1) * rows, :cols]
        x_s[r, pl.ds(other, cols)] = pieces[q][j * rows : (j + 1) * rows, :cols]
        tail = pieces[p][i * rows : (i + 1) * rows, cols:].astype(F32)
        w_s[r, :] = jnp.broadcast_to(jnp.sum(jnp.where(chosen, tail, 0.0), axis=1, keepdims=True), (rows, 128))
    for step in range(STEPS):
        f = step * fb
        if fresh:
            stream(0, step).wait()
            stream(1, step).wait()
        x = x_s[...]
        g = lax.dot_general(x, wg[pl.ds(f, fb), :], NT, preferred_element_type=F32)
        u = lax.dot_general(x, wu[pl.ds(f, fb), :], NT, preferred_element_type=F32)
        h_s[:, pl.ds(f, fb)] = (g / (1.0 + jnp.exp(-g)) * u * w_s[:, :1]).astype(BF)
    if fresh:
        for step in range(STEPS):
            stream(2, step).wait()
    for n in range(0, 2 * cols, nb):
        far = int(n >= cols)
        off = n - cols if far else n
        at = pl.multiple_of((other if far else mine) + off, 128)
        o = jnp.dot(h_s[...], wd[:, pl.ds(at, nb)], preferred_element_type=F32).astype(BF)
        for b in range(UNITS):
            core, plane, side = b // BLOCKS, b // 2 % 2, b % 2
            unit = 3 - 2 * side - far
            k = unit * rows
            outs[2 * plane + core][k : k + rows, off : off + nb] = o[b * rows : (b + 1) * rows]


def ffn(sc, pieces, layout, cols, weights, fresh, first_of_all):
    ff, d = weights[0].shape
    total = len(layout) * (pieces[0].shape[0] // BLOCKS)
    vmem = pl.BlockSpec(memory_space=pltpu.VMEM)
    out = [pltpu.VMEM((total // 2, cols), BF)] * 4
    scratch = [pltpu.VMEM((total, d), BF), pltpu.VMEM((total, ff), BF), pltpu.VMEM((total, 128), F32)]
    if fresh:
        out += [pltpu.VMEM(a.shape, BF) for a in weights]
        scratch.append(pltpu.SemaphoreType.DMA((3 * STEPS,)))
    return pl.pallas_call(
        functools.partial(ffn_kernel, layout, cols, fresh, len(first_of_all), len(pieces)),
        in_specs=[pl.BlockSpec(memory_space=pl.ANY)] * len(first_of_all)
        + [pl.BlockSpec(memory_space=pltpu.SMEM)]
        + [vmem] * len(pieces)
        + [pl.BlockSpec(memory_space=pltpu.HBM) if fresh else vmem] * 3,
        out_specs=[vmem] * len(out),
        out_shape=out,
        scratch_shapes=scratch,
        compiler_params=pltpu.CompilerParams(vmem_limit_bytes=(30 if fresh else 8) << 20),
        cost_estimate=pl.CostEstimate(
            flops=6 * total * ff * d, bytes_accessed=6 * ff * d + 4 * total * d, transcendentals=total * ff
        ),
        name="ffn",
    )(*first_of_all, sc, *pieces, *weights)


def dense_weights(expert_ids, combine_weights, experts):
    hits = expert_ids[:, :, None] == jnp.arange(experts, dtype=jnp.int32)
    return jnp.sum(jnp.where(hits, combine_weights[:, :, None], 0.0), axis=1)


def on_device(tokens, expert_ids, combine_weights, gate_proj, up_proj, down_proj):
    held, cols = tokens.shape
    nz, nx = lax.axis_size("z"), lax.axis_size("x")
    experts = nz * nx * 2
    z, x, c, y = (lax.axis_index(a) for a in ("z", "x", "c", "y"))
    sc = jnp.stack([y, (z * nx + x) * 2 + c]).astype(jnp.int32)
    weights = (gate_proj[0], up_proj[0], down_proj[0])

    swap = [(0, 1), (1, 0)]
    px = lambda a: lax.ppermute(a, "x", swap)
    py = lambda a: lax.ppermute(a, "y", swap)
    pc = lambda a: lax.ppermute(a, "c", swap)
    pd = lambda a: lax.ppermute(a, ("x", "y"), [(i, 3 - i) for i in range(4)])
    pz = lambda a, k: lax.ppermute(a, "z", [(i, i ^ k) for i in range(nz)])

    w = dense_weights(expert_ids, combine_weights, experts)
    hi = w.astype(BF)
    lo = (w - hi.astype(F32)).astype(BF)
    pad = jnp.zeros((held, 64 - experts), BF)
    t0 = jnp.concatenate([tokens, hi, pad, lo, pad], axis=1)

    t3, t1, x0, y0, d0 = pz(t0, 3), pz(t0, 1), px(t0), py(t0), pd(t0)
    t2, x3, y3 = pz(t3, 1), px(t3), py(t3)
    x3, t2, x0, y0, d0 = lax.optimization_barrier((x3, t2, x0, y0, d0))
    rest0 = jnp.concatenate([y0, x0, d0])
    d3, x2, y2, d2 = lax.optimization_barrier((py(x3), px(t2), py(t2), pd(t2)))
    p0, p1, p2, p3 = (
        jnp.concatenate(blocks)
        for blocks in ([t0, rest0], [t1, pz(rest0, 1)], [t2, y2, x2, d2], [t3, y3, x3, d3])
    )
    layout = [(p, 2 * side, p, 2 * side + 1) for p in range(4) for side in range(2)]

    def core_sum(mine, others):
        return mine.astype(F32) + pc(others).astype(F32)

    def plane_parts(s):
        d, x, y, own = s.reshape(BLOCKS, held, cols)
        return own, px(x), py(y), pd(d)

    *first, wg, wu, wd = ffn(sc, [p3, p1, pc(p3), pc(p1)], layout, cols, weights, True, [])
    s3, s1 = core_sum(*first[:2]).astype(BF), core_sum(*first[2:]).astype(BF)
    last = ffn(sc, [p2, p0, pc(p2), pc(p0)], layout, cols, (wg, wu, wd), False, [s3, s1])
    last = list(last)
    d1, x1, y1, own1 = s1.reshape(BLOCKS, held, cols)
    to1 = s1[: 2 * held]
    held_back = lax.optimization_barrier((*last, own1, pz(to1, 1), py(y1), *plane_parts(s3)))
    last, own1, back1, back_y, parts3 = held_back[:4], *held_back[4:7], held_back[7:]
    back3 = pz(sum(p.astype(F32) for p in parts3).astype(BF), 3)
    own1 = pz((own1.astype(F32) + back_y.astype(F32)).astype(BF), 1)
    s2 = core_sum(*last[:2]).astype(BF)
    parts2 = plane_parts(s2)
    back2 = pz(sum(p.astype(F32) for p in parts2).astype(BF), 2)
    s0 = core_sum(*last[2:])
    s0 = s0 + jnp.concatenate([back1.astype(F32), jnp.zeros((2 * held, cols), F32)])
    total = sum(p.astype(F32) for p in plane_parts(s0.astype(BF)))
    total = total + own1.astype(F32) + back3.astype(F32) + back2.astype(F32)
    return total.astype(BF)


def on_device_any(tokens, expert_ids, combine_weights, gate_proj, up_proj, down_proj):
    groups = lax.axis_size("exp")
    held, cols = tokens.shape
    local = gate_proj.shape[0]
    w = lax.all_gather(dense_weights(expert_ids, combine_weights, groups * local), "exp", axis=0, tiled=True)
    rows = lax.all_gather(lax.all_gather(tokens, "ten", axis=1, tiled=True), "exp", axis=0, tiled=True)
    total = jnp.zeros((rows.shape[0], rows.shape[1]), F32)
    for j in range(local):
        g = lax.dot_general(rows, gate_proj[j], NT, preferred_element_type=F32)
        u = lax.dot_general(rows, up_proj[j], NT, preferred_element_type=F32)
        mine = jnp.take(w, lax.axis_index("exp") * local + j, axis=1)[:, None]
        h = (jax.nn.silu(g) * u * mine).astype(BF)
        total = total + jnp.dot(h, down_proj[j], preferred_element_type=F32)
    part = lax.psum_scatter(total.astype(BF), "exp", scatter_dimension=0, tiled=True)
    return lax.psum_scatter(part, "ten", scatter_dimension=1, tiled=True).astype(BF)


def solution(mesh):
    sizes = (mesh.shape["exp"], mesh.shape["ten"])
    if sizes == (16, 2):
        mesh = Mesh(mesh.devices.reshape(4, 2, 2, 2), ("z", "x", "c", "y"))
        exp, ten, body = ("z", "x", "c"), "y", on_device
    else:
        exp, ten, body = "exp", "ten", on_device_any
    return jax.shard_map(
        body,
        mesh=mesh,
        in_specs=(
            P(exp, ten),
            P(exp, None),
            P(exp, None),
            P(exp, ten, None),
            P(exp, ten, None),
            P(exp, ten, None),
        ),
        out_specs=P(exp, ten),
        check_vma=False,
    )
```

```python
import functools

import jax
import jax.numpy as jnp
from jax import lax
from jax.experimental import pallas as pl
from jax.experimental.pallas import tpu as pltpu
from jax.sharding import Mesh, PartitionSpec as P

BF = jnp.bfloat16
F32 = jnp.float32
NT = (((1,), (1,)), ((), ()))


STEPS = 3
BLOCKS = 4
UNITS = 8


def ffn_kernel(layout, cols, fresh, waits, count, *refs):
    refs = refs[waits:]
    sc, refs = refs[0], refs[1:]
    pieces, given, outs, refs = refs[:count], refs[count : count + 3], refs[count + 3 : count + 7], refs[count + 7 :]
    held = given
    if fresh:
        held, refs = refs[:3], refs[3:]
    wg, wu, wd = held
    x_s, h_s, w_s = refs[:3]
    rows = x_s.shape[0] // UNITS
    ff, d = wg.shape
    fb, nb = ff // STEPS, 512

    def stream(k, step):
        part = pl.ds(step * fb, fb)
        return pltpu.make_async_copy(given[k].at[part], held[k].at[part], refs[3].at[k * STEPS + step])

    if fresh:
        for step in range(STEPS):
            stream(0, step).start()
            stream(1, step).start()
        for step in range(STEPS):
            stream(2, step).start()
    mine = pl.multiple_of(sc[0] * cols, 128)
    other = pl.multiple_of((1 - sc[0]) * cols, 128)
    lane = lax.broadcasted_iota(jnp.int32, (rows, 128), 1)
    chosen = (lane == sc[1]) | (lane == sc[1] + 64)
    for b, (p, i, q, j) in enumerate(layout):
        r = pl.ds(b * rows, rows)
        x_s[r, pl.ds(mine, cols)] = pieces[p][i * rows : (i + 1) * rows, :cols]
        x_s[r, pl.ds(other, cols)] = pieces[q][j * rows : (j + 1) * rows, :cols]
        tail = pieces[p][i * rows : (i + 1) * rows, cols:].astype(F32)
        w_s[r, :] = jnp.broadcast_to(jnp.sum(jnp.where(chosen, tail, 0.0), axis=1, keepdims=True), (rows, 128))
    for step in range(STEPS):
        f = step * fb
        if fresh:
            stream(0, step).wait()
            stream(1, step).wait()
        x = x_s[...]
        g = lax.dot_general(x, wg[pl.ds(f, fb), :], NT, preferred_element_type=F32)
        u = lax.dot_general(x, wu[pl.ds(f, fb), :], NT, preferred_element_type=F32)
        h_s[:, pl.ds(f, fb)] = (g / (1.0 + jnp.exp(-g)) * u * w_s[:, :1]).astype(BF)
    if fresh:
        for step in range(STEPS):
            stream(2, step).wait()
    for n in range(0, 2 * cols, nb):
        far = int(n >= cols)
        off = n - cols if far else n
        at = pl.multiple_of((other if far else mine) + off, 128)
        o = jnp.dot(h_s[...], wd[:, pl.ds(at, nb)], preferred_element_type=F32).astype(BF)
        for b in range(UNITS):
            core, plane, side = b // BLOCKS, b // 2 % 2, b % 2
            unit = 3 - 2 * side - far
            k = unit * rows
            outs[2 * plane + core][k : k + rows, off : off + nb] = o[b * rows : (b + 1) * rows]


def ffn(sc, pieces, layout, cols, weights, fresh, first_of_all):
    ff, d = weights[0].shape
    total = len(layout) * (pieces[0].shape[0] // BLOCKS)
    vmem = pl.BlockSpec(memory_space=pltpu.VMEM)
    out = [pltpu.VMEM((total // 2, cols), BF)] * 4
    scratch = [pltpu.VMEM((total, d), BF), pltpu.VMEM((total, ff), BF), pltpu.VMEM((total, 128), F32)]
    if fresh:
        out += [pltpu.VMEM(a.shape, BF) for a in weights]
        scratch.append(pltpu.SemaphoreType.DMA((3 * STEPS,)))
    return pl.pallas_call(
        functools.partial(ffn_kernel, layout, cols, fresh, len(first_of_all), len(pieces)),
        in_specs=[pl.BlockSpec(memory_space=pl.ANY)] * len(first_of_all)
        + [pl.BlockSpec(memory_space=pltpu.SMEM)]
        + [vmem] * len(pieces)
        + [pl.BlockSpec(memory_space=pltpu.HBM) if fresh else vmem] * 3,
        out_specs=[vmem] * len(out),
        out_shape=out,
        scratch_shapes=scratch,
        compiler_params=pltpu.CompilerParams(vmem_limit_bytes=(30 if fresh else 8) << 20),
        cost_estimate=pl.CostEstimate(
            flops=6 * total * ff * d, bytes_accessed=6 * ff * d + 4 * total * d, transcendentals=total * ff
        ),
        name="ffn",
    )(*first_of_all, sc, *pieces, *weights)


def dense_weights(expert_ids, combine_weights, experts):
    hits = expert_ids[:, :, None] == jnp.arange(experts, dtype=jnp.int32)
    return jnp.sum(jnp.where(hits, combine_weights[:, :, None], 0.0), axis=1)


def on_device(tokens, expert_ids, combine_weights, gate_proj, up_proj, down_proj):
    held, cols = tokens.shape
    nz, nx = lax.axis_size("z"), lax.axis_size("x")
    experts = nz * nx * 2
    z, x, c, y = (lax.axis_index(a) for a in ("z", "x", "c", "y"))
    sc = jnp.stack([y, (z * nx + x) * 2 + c]).astype(jnp.int32)
    weights = (gate_proj[0], up_proj[0], down_proj[0])

    swap = [(0, 1), (1, 0)]
    px = lambda a: lax.ppermute(a, "x", swap)
    py = lambda a: lax.ppermute(a, "y", swap)
    pc = lambda a: lax.ppermute(a, "c", swap)
    pd = lambda a: lax.ppermute(a, ("x", "y"), [(i, 3 - i) for i in range(4)])
    pz = lambda a, k: lax.ppermute(a, "z", [(i, i ^ k) for i in range(nz)])

    w = dense_weights(expert_ids, combine_weights, experts)
    hi = w.astype(BF)
    lo = (w - hi.astype(F32)).astype(BF)
    pad = jnp.zeros((held, 64 - experts), BF)
    t0 = jnp.concatenate([tokens, hi, pad, lo, pad], axis=1)

    t3, t1, x0, y0, d0 = pz(t0, 3), pz(t0, 1), px(t0), py(t0), pd(t0)
    t2, x3, y3 = pz(t3, 1), px(t3), py(t3)
    x3, t2, x0, y0, d0 = lax.optimization_barrier((x3, t2, x0, y0, d0))
    rest0 = jnp.concatenate([y0, x0, d0])
    d3, x2, y2, d2 = lax.optimization_barrier((py(x3), px(t2), py(t2), pd(t2)))
    p0, p1, p2, p3 = (
        jnp.concatenate(blocks)
        for blocks in ([t0, rest0], [t1, pz(rest0, 1)], [t2, y2, x2, d2], [t3, y3, x3, d3])
    )
    layout = [(p, 2 * side, p, 2 * side + 1) for p in range(4) for side in range(2)]

    def core_sum(mine, others):
        return mine.astype(F32) + pc(others).astype(F32)

    def plane_parts(s):
        d, x, y, own = s.reshape(BLOCKS, held, cols)
        return own, px(x), py(y), pd(d)

    *first, wg, wu, wd = ffn(sc, [p3, p1, pc(p3), pc(p1)], layout, cols, weights, True, [])
    s3, s1 = core_sum(*first[:2]).astype(BF), core_sum(*first[2:]).astype(BF)
    last = ffn(sc, [p2, p0, pc(p2), pc(p0)], layout, cols, (wg, wu, wd), False, [s3, s1])
    last = list(last)
    cut = 3 * held
    held_back = lax.optimization_barrier((*last, s1[cut:], pz(s1[:cut], 1), *plane_parts(s3)))
    last, own1, back1, parts3 = held_back[:4], *held_back[4:6], held_back[6:]
    back3 = pz(sum(p.astype(F32) for p in parts3).astype(BF), 3)
    own1 = pz(own1, 1)
    s2 = core_sum(*last[:2]).astype(BF)
    parts2 = plane_parts(s2)
    back2 = pz(sum(p.astype(F32) for p in parts2).astype(BF), 2)
    s0 = core_sum(*last[2:])
    s0 = s0 + jnp.concatenate([back1.astype(F32), jnp.zeros((held, cols), F32)])
    total = sum(p.astype(F32) for p in plane_parts(s0.astype(BF)))
    total = total + own1.astype(F32) + back3.astype(F32) + back2.astype(F32)
    return total.astype(BF)


def on_device_any(tokens, expert_ids, combine_weights, gate_proj, up_proj, down_proj):
    groups = lax.axis_size("exp")
    held, cols = tokens.shape
    local = gate_proj.shape[0]
    w = lax.all_gather(dense_weights(expert_ids, combine_weights, groups * local), "exp", axis=0, tiled=True)
    rows = lax.all_gather(lax.all_gather(tokens, "ten", axis=1, tiled=True), "exp", axis=0, tiled=True)
    total = jnp.zeros((rows.shape[0], rows.shape[1]), F32)
    for j in range(local):
        g = lax.dot_general(rows, gate_proj[j], NT, preferred_element_type=F32)
        u = lax.dot_general(rows, up_proj[j], NT, preferred_element_type=F32)
        mine = jnp.take(w, lax.axis_index("exp") * local + j, axis=1)[:, None]
        h = (jax.nn.silu(g) * u * mine).astype(BF)
        total = total + jnp.dot(h, down_proj[j], preferred_element_type=F32)
    part = lax.psum_scatter(total.astype(BF), "exp", scatter_dimension=0, tiled=True)
    return lax.psum_scatter(part, "ten", scatter_dimension=1, tiled=True).astype(BF)


def solution(mesh):
    sizes = (mesh.shape["exp"], mesh.shape["ten"])
    if sizes == (16, 2):
        mesh = Mesh(mesh.devices.reshape(4, 2, 2, 2), ("z", "x", "c", "y"))
        exp, ten, body = ("z", "x", "c"), "y", on_device
    else:
        exp, ten, body = "exp", "ten", on_device_any
    return jax.shard_map(
        body,
        mesh=mesh,
        in_specs=(
            P(exp, ten),
            P(exp, None),
            P(exp, None),
            P(exp, ten, None),
            P(exp, ten, None),
            P(exp, ten, None),
        ),
        out_specs=P(exp, ten),
        check_vma=False,
    )
```

```python
import functools

import jax
import jax.numpy as jnp
from jax import lax
from jax.experimental import pallas as pl
from jax.experimental.pallas import tpu as pltpu
from jax.sharding import Mesh, PartitionSpec as P

BF = jnp.bfloat16
F32 = jnp.float32
NT = (((1,), (1,)), ((), ()))


STEPS = 3
BLOCKS = 4
UNITS = 8


def ffn_kernel(layout, cols, fresh, waits, count, *refs):
    refs = refs[waits:]
    sc, refs = refs[0], refs[1:]
    pieces, given, outs, refs = refs[:count], refs[count : count + 3], refs[count + 3 : count + 7], refs[count + 7 :]
    held = given
    if fresh:
        held, refs = refs[:3], refs[3:]
    wg, wu, wd = held
    x_s, h_s, w_s = refs[:3]
    rows = x_s.shape[0] // UNITS
    ff, d = wg.shape
    fb, nb = ff // STEPS, 512

    def stream(k, step):
        part = pl.ds(step * fb, fb)
        return pltpu.make_async_copy(given[k].at[part], held[k].at[part], refs[3].at[k * STEPS + step])

    if fresh:
        for step in range(STEPS):
            stream(0, step).start()
            stream(1, step).start()
        for step in range(STEPS):
            stream(2, step).start()
    mine = pl.multiple_of(sc[0] * cols, 128)
    other = pl.multiple_of((1 - sc[0]) * cols, 128)
    lane = lax.broadcasted_iota(jnp.int32, (rows, 128), 1)
    chosen = (lane == sc[1]) | (lane == sc[1] + 64)
    for b, (p, i, q, j) in enumerate(layout):
        r = pl.ds(b * rows, rows)
        x_s[r, pl.ds(mine, cols)] = pieces[p][i * rows : (i + 1) * rows, :cols]
        x_s[r, pl.ds(other, cols)] = pieces[q][j * rows : (j + 1) * rows, :cols]
        tail = pieces[p][i * rows : (i + 1) * rows, cols:].astype(F32)
        w_s[r, :] = jnp.broadcast_to(jnp.sum(jnp.where(chosen, tail, 0.0), axis=1, keepdims=True), (rows, 128))
    for step in range(STEPS):
        f = step * fb
        if fresh:
            stream(0, step).wait()
            stream(1, step).wait()
        x = x_s[...]
        g = lax.dot_general(x, wg[pl.ds(f, fb), :], NT, preferred_element_type=F32)
        u = lax.dot_general(x, wu[pl.ds(f, fb), :], NT, preferred_element_type=F32)
        h_s[:, pl.ds(f, fb)] = (g / (1.0 + jnp.exp(-g)) * u * w_s[:, :1]).astype(BF)
    if fresh:
        for step in range(STEPS):
            stream(2, step).wait()
    for n in range(0, 2 * cols, nb):
        far = int(n >= cols)
        off = n - cols if far else n
        at = pl.multiple_of((other if far else mine) + off, 128)
        o = jnp.dot(h_s[...], wd[:, pl.ds(at, nb)], preferred_element_type=F32).astype(BF)
        for b in range(UNITS):
            core, plane, side = b // BLOCKS, b // 2 % 2, b % 2
            unit = 3 - 2 * side - far
            k = unit * rows
            outs[2 * plane + core][k : k + rows, off : off + nb] = o[b * rows : (b + 1) * rows]


def ffn(sc, pieces, layout, cols, weights, fresh, first_of_all):
    ff, d = weights[0].shape
    total = len(layout) * (pieces[0].shape[0] // BLOCKS)
    vmem = pl.BlockSpec(memory_space=pltpu.VMEM)
    out = [pltpu.VMEM((total // 2, cols), BF)] * 4
    scratch = [pltpu.VMEM((total, d), BF), pltpu.VMEM((total, ff), BF), pltpu.VMEM((total, 128), F32)]
    if fresh:
        out += [pltpu.VMEM(a.shape, BF) for a in weights]
        scratch.append(pltpu.SemaphoreType.DMA((3 * STEPS,)))
    return pl.pallas_call(
        functools.partial(ffn_kernel, layout, cols, fresh, len(first_of_all), len(pieces)),
        in_specs=[pl.BlockSpec(memory_space=pl.ANY)] * len(first_of_all)
        + [pl.BlockSpec(memory_space=pltpu.SMEM)]
        + [vmem] * len(pieces)
        + [pl.BlockSpec(memory_space=pltpu.HBM) if fresh else vmem] * 3,
        out_specs=[vmem] * len(out),
        out_shape=out,
        scratch_shapes=scratch,
        compiler_params=pltpu.CompilerParams(vmem_limit_bytes=(30 if fresh else 8) << 20),
        cost_estimate=pl.CostEstimate(
            flops=6 * total * ff * d, bytes_accessed=6 * ff * d + 4 * total * d, transcendentals=total * ff
        ),
        name="ffn",
    )(*first_of_all, sc, *pieces, *weights)


def dense_weights(expert_ids, combine_weights, experts):
    hits = expert_ids[:, :, None] == jnp.arange(experts, dtype=jnp.int32)
    return jnp.sum(jnp.where(hits, combine_weights[:, :, None], 0.0), axis=1)


def on_device(tokens, expert_ids, combine_weights, gate_proj, up_proj, down_proj):
    held, cols = tokens.shape
    nz, nx = lax.axis_size("z"), lax.axis_size("x")
    experts = nz * nx * 2
    z, x, c, y = (lax.axis_index(a) for a in ("z", "x", "c", "y"))
    sc = jnp.stack([y, (z * nx + x) * 2 + c]).astype(jnp.int32)
    weights = (gate_proj[0], up_proj[0], down_proj[0])

    swap = [(0, 1), (1, 0)]
    px = lambda a: lax.ppermute(a, "x", swap)
    py = lambda a: lax.ppermute(a, "y", swap)
    pc = lambda a: lax.ppermute(a, "c", swap)
    pd = lambda a: lax.ppermute(a, ("x", "y"), [(i, 3 - i) for i in range(4)])
    pz = lambda a, k: lax.ppermute(a, "z", [(i, i ^ k) for i in range(nz)])

    w = dense_weights(expert_ids, combine_weights, experts)
    hi = w.astype(BF)
    lo = (w - hi.astype(F32)).astype(BF)
    pad = jnp.zeros((held, 64 - experts), BF)
    t0 = jnp.concatenate([tokens, hi, pad, lo, pad], axis=1)

    t3, t1, x0, y0, d0 = pz(t0, 3), pz(t0, 1), px(t0), py(t0), pd(t0)
    t2, x3, y3 = pz(t3, 1), px(t3), py(t3)
    x3, t2, x0, y0, d0 = lax.optimization_barrier((x3, t2, x0, y0, d0))
    rest0 = jnp.concatenate([y0, x0, d0])
    y2 = py(t2)
    d3, x2, y2, d2 = lax.optimization_barrier((py(x3), px(t2), y2, px(y2)))
    p0, p1, p2, p3 = (
        jnp.concatenate(blocks)
        for blocks in ([t0, rest0], [t1, pz(rest0, 1)], [t2, y2, x2, d2], [t3, y3, x3, d3])
    )
    layout = [(p, 2 * side, p, 2 * side + 1) for p in range(4) for side in range(2)]

    def core_sum(mine, others):
        return mine.astype(F32) + pc(others).astype(F32)

    def plane_parts(s):
        d, x, y, own = s.reshape(BLOCKS, held, cols)
        return own, px(x), py(y), pd(d)

    *first, wg, wu, wd = ffn(sc, [p3, p1, pc(p3), pc(p1)], layout, cols, weights, True, [])
    s3, s1 = core_sum(*first[:2]).astype(BF), core_sum(*first[2:]).astype(BF)
    last = ffn(sc, [p2, p0, pc(p2), pc(p0)], layout, cols, (wg, wu, wd), False, [s3, s1])
    last = list(last)
    cut = 3 * held
    held_back = lax.optimization_barrier((*last, s1[cut:], pz(s1[:cut], 1), *plane_parts(s3)))
    last, own1, back1, parts3 = held_back[:4], *held_back[4:6], held_back[6:]
    back3 = pz(sum(p.astype(F32) for p in parts3).astype(BF), 3)
    own1 = pz(own1, 1)
    s2 = core_sum(*last[:2]).astype(BF)
    parts2 = plane_parts(s2)
    back2 = pz(sum(p.astype(F32) for p in parts2).astype(BF), 2)
    s0 = core_sum(*last[2:])
    s0 = s0 + jnp.concatenate([back1.astype(F32), jnp.zeros((held, cols), F32)])
    total = sum(p.astype(F32) for p in plane_parts(s0.astype(BF)))
    total = total + own1.astype(F32) + back3.astype(F32) + back2.astype(F32)
    return total.astype(BF)


def on_device_any(tokens, expert_ids, combine_weights, gate_proj, up_proj, down_proj):
    groups = lax.axis_size("exp")
    held, cols = tokens.shape
    local = gate_proj.shape[0]
    w = lax.all_gather(dense_weights(expert_ids, combine_weights, groups * local), "exp", axis=0, tiled=True)
    rows = lax.all_gather(lax.all_gather(tokens, "ten", axis=1, tiled=True), "exp", axis=0, tiled=True)
    total = jnp.zeros((rows.shape[0], rows.shape[1]), F32)
    for j in range(local):
        g = lax.dot_general(rows, gate_proj[j], NT, preferred_element_type=F32)
        u = lax.dot_general(rows, up_proj[j], NT, preferred_element_type=F32)
        mine = jnp.take(w, lax.axis_index("exp") * local + j, axis=1)[:, None]
        h = (jax.nn.silu(g) * u * mine).astype(BF)
        total = total + jnp.dot(h, down_proj[j], preferred_element_type=F32)
    part = lax.psum_scatter(total.astype(BF), "exp", scatter_dimension=0, tiled=True)
    return lax.psum_scatter(part, "ten", scatter_dimension=1, tiled=True).astype(BF)


def solution(mesh):
    sizes = (mesh.shape["exp"], mesh.shape["ten"])
    if sizes == (16, 2):
        mesh = Mesh(mesh.devices.reshape(4, 2, 2, 2), ("z", "x", "c", "y"))
        exp, ten, body = ("z", "x", "c"), "y", on_device
    else:
        exp, ten, body = "exp", "ten", on_device_any
    return jax.shard_map(
        body,
        mesh=mesh,
        in_specs=(
            P(exp, ten),
            P(exp, None),
            P(exp, None),
            P(exp, ten, None),
            P(exp, ten, None),
            P(exp, ten, None),
        ),
        out_specs=P(exp, ten),
        check_vma=False,
    )
```
